1024 devices in a mesh: replica: 32 (over z_lo, y, core), mp: 32 (over x, z_hi).
Axes of the slice: x: 8, y: 8, z: 8 (z_hi: 4, z_lo: 2; z = z_hi * 2 + z_lo), core: 2. Of those that a mesh axis runs over, the one named last changes fastest.
Arguments:
- code_table: int32 [16], replicated, may hold values from -7 to 7
- up_codes: int32 [32, 2, 32, 28672], P('replica', None, None, 'mp'), may hold values from 0 to 15
- up_exps: int32 [32, 2, 32, 224], P('replica', None, None, 'mp'), may hold values from -8 to -3
- up_global: float32 [2, 32, 28672], P(None, 'replica', 'mp'), may hold values from -6 to 6
- up_moment: float32 [2, 32, 28672], P(None, 'replica', 'mp'), may hold values from -4 to 4
- up_local: bfloat16 [32, 2, 32, 28672], P('replica', None, None, 'mp'), may hold values from -6 to 6
- down_codes: int32 [32, 32, 8192], P('replica', None, 'mp'), may hold values from 0 to 15
- down_exps: int32 [32, 32, 64], P('replica', None, 'mp'), may hold values from -8 to -3
- down_global: float32 [32, 8192], P('replica', 'mp'), may hold values from -6 to 6
- down_moment: float32 [32, 8192], P('replica', 'mp'), may hold values from -4 to 4
- down_local: bfloat16 [32, 32, 8192], P('replica', None, 'mp'), may hold values from -6 to 6
Outputs:
- up_global_new: float32 [2, 32, 28672], P(None, 'replica', 'mp')
- up_moment_new: float32 [2, 32, 28672], P(None, 'replica', 'mp')
- up_merged: bfloat16 [32, 2, 32, 28672], P('replica', None, None, 'mp')
- down_global_new: float32 [32, 8192], P('replica', 'mp')
- down_moment_new: float32 [32, 8192], P('replica', 'mp')
- down_merged: bfloat16 [32, 32, 8192], P('replica', None, 'mp')
The draws below stay inside these ranges and needn't reach their ends.
All inputs are finite; a program needn't handle non-finite values.
Results may differ from the reference program's by a relative error of at most 0.0044.
Values may be sent and summed in bfloat16 or wider, within the bound.
No kernel may reach another device: no remote copies, remote signals or barrier semaphores. Data moves between devices by JAX's collectives and lax.ppermute only.
A program may use at most 32 MiB of HBM per device.

```python
import jax
import jax.numpy as jnp
from jax import lax

D = 8192
FF = 28672
BLOCK = 128
REPLICAS = 32
ROWS = 32


def touch_ends(drawn, key, smallest, largest):
    dims = drawn.shape
    index_at = [jax.random.randint(jax.random.fold_in(key, axis), (), 0, dims[axis]) for axis in range(len(dims))]
    drawn = drawn.at[tuple(index_at)].set(smallest)
    longest = dims.index(max(dims))
    index_at[longest] = (index_at[longest] + 1) % dims[longest]
    return drawn.at[tuple(index_at)].set(largest)


def steps_of(rng, shape, pieces, low, largest):
    def one(dim, shards_of):
        steps = jax.random.uniform(jax.random.fold_in(jax.random.fold_in(rng, 6), dim), (shards_of,), jnp.float32, low / len(pieces), largest / len(pieces))
        return jnp.repeat(jnp.exp(steps), shape[dim] // shards_of).reshape((-1,) + (1,) * (len(shape) - dim - 1))

    level = one(*pieces[0])
    for cut in pieces[1:]:
        level = level * one(*cut)
    return level


def noise(key, dims, scale, limit, cuts=(), dtype=jnp.bfloat16):
    gain = steps_of(key, dims, cuts, -0.22, 0.18) if cuts else 1.0
    values = jax.random.normal(key, dims, jnp.float32) * scale * gain
    return jnp.minimum(jnp.maximum(values, -limit), limit).astype(dtype)


def setup_inputs(seed: int = 0) -> dict:
    arg_keys = jax.random.split(jax.random.key(seed), 12)
    code_table = touch_ends(jax.random.randint(arg_keys[0], (16,), -7, 8), jax.random.fold_in(arg_keys[0], 1), -7, 7).astype(jnp.int32)
    up_codes = touch_ends(jax.random.randint(arg_keys[1], (REPLICAS, 2, ROWS, FF), 0, 16), jax.random.fold_in(arg_keys[1], 1), 0, 15).astype(jnp.int32)
    up_exps = touch_ends(jax.random.randint(arg_keys[2], (REPLICAS, 2, ROWS, FF // BLOCK), -8, -2), jax.random.fold_in(arg_keys[2], 1), -8, (-2) - 1).astype(jnp.int32)
    up_global = noise(arg_keys[3], (2, ROWS, FF), 1.0, 6.0, ((1, 32), (2, 32)), jnp.float32)
    up_moment = noise(arg_keys[4], (2, ROWS, FF), 0.5, 4.0, ((1, 32), (2, 32)), jnp.float32)
    up_local = noise(arg_keys[5], (REPLICAS, 2, ROWS, FF), 1.0, 6.0, ((0, 32), (3, 32)))
    down_codes = touch_ends(jax.random.randint(arg_keys[6], (REPLICAS, ROWS, D), 0, 16), jax.random.fold_in(arg_keys[6], 1), 0, 15).astype(jnp.int32)
    down_exps = touch_ends(jax.random.randint(arg_keys[7], (REPLICAS, ROWS, D // BLOCK), -8, -2), jax.random.fold_in(arg_keys[7], 1), -8, (-2) - 1).astype(jnp.int32)
    down_global = noise(arg_keys[8], (ROWS, D), 1.0, 6.0, ((0, 32), (1, 32)), jnp.float32)
    down_moment = noise(arg_keys[9], (ROWS, D), 0.5, 4.0, ((0, 32), (1, 32)), jnp.float32)
    down_local = noise(arg_keys[10], (REPLICAS, ROWS, D), 1.0, 6.0, ((0, 32), (2, 32)))
    return {"code_table": code_table, "up_codes": up_codes, "up_exps": up_exps, "up_global": up_global, "up_moment": up_moment, "up_local": up_local, "down_codes": down_codes, "down_exps": down_exps, "down_global": down_global, "down_moment": down_moment, "down_local": down_local}


outer_rate = 0.7
nesterov = 0.9
mixing = 0.5


def decode(codes, exps, code_table):
    values = jnp.take(code_table.astype(jnp.float32), codes, axis=0)
    scales = jnp.exp2(exps.astype(jnp.float32))
    scales = jnp.repeat(scales, BLOCK, axis=-1)
    return (values * scales).astype(jnp.bfloat16)


def outer_step(code_table, codes, exps, weights, moment, local):
    def add_one(total, pair):
        return total + decode(pair[0], pair[1], code_table).astype(jnp.float32), None

    total, _ = lax.scan(add_one, jnp.zeros(weights.shape, jnp.float32), (codes, exps))
    mean = total / REPLICAS
    moment_new = nesterov * moment + mean
    weights_new = weights - outer_rate * (mean + nesterov * moment_new)
    shared = weights_new.astype(jnp.bfloat16).astype(jnp.float32)
    merged = (mixing * local.astype(jnp.float32) + (1.0 - mixing) * shared[None]).astype(jnp.bfloat16)
    return weights_new, moment_new, merged


def reference(code_table, up_codes, up_exps, up_global, up_moment, up_local, down_codes, down_exps, down_global, down_moment, down_local):
    up_new, up_mom, up_merged = outer_step(code_table, up_codes, up_exps, up_global, up_moment, up_local)
    down_new, down_mom, down_merged = outer_step(code_table, down_codes, down_exps, down_global, down_moment, down_local)
    return (up_new, up_mom, up_merged, down_new, down_mom, down_merged)
```

```python
import jax
import jax.numpy as jnp
from jax import lax
from jax.experimental import pallas as pl
from jax.experimental.pallas import tpu as pltpu
from jax.sharding import PartitionSpec as P

LANES = 128
LOW_EXP = -8

outer_rate = 0.7
nesterov = 0.9
mixing = 0.5

VMEM = pl.BlockSpec(memory_space=pltpu.VMEM)
SMEM = pl.BlockSpec(memory_space=pltpu.SMEM)


def up_slots(groups, blocks):
    return [(s * groups + g, g, s) for s in range(blocks) for g in range(groups)]


def decode_kernel(table_ref, up_codes, up_exps, down_codes, down_exps, out_ref, codes_by_row, exps_by_slot):
    groups, rows, width = up_codes.shape
    up_blocks = width // LANES
    down_blocks = down_codes.shape[1] // LANES
    slots = groups * up_blocks + down_blocks
    for j, g, s in up_slots(groups, up_blocks):
        codes_by_row[pl.ds(j, rows, stride=slots), :] = up_codes[g, :, s * LANES : (s + 1) * LANES]
        exps_by_slot[j : j + 1, :] = up_exps[s, g : g + 1, :]
    for t in range(down_blocks):
        j = groups * up_blocks + t
        codes_by_row[pl.ds(j, rows, stride=slots), :] = down_codes[:, t * LANES : (t + 1) * LANES]
        exps_by_slot[j : j + 1, :] = down_exps[t : t + 1, :]
    lane = lax.broadcasted_iota(jnp.int32, (slots, LANES), 1)
    table = jnp.zeros((slots, LANES), jnp.int32)
    for level in range(16):
        table = jnp.where(lane == level, table_ref[level], table)
    scales = jnp.left_shift(1, exps_by_slot[...] - LOW_EXP).astype(jnp.float32) * 2.0**LOW_EXP
    table = table.astype(jnp.float32)
    for r in range(rows):
        codes = codes_by_row[r * slots : (r + 1) * slots, :]
        values = jnp.take_along_axis(table, codes, axis=1)
        out_ref[r] = (values * scales[:, r : r + 1]).astype(jnp.bfloat16)


def advance_kernel(
    recv, up_global, up_moment, down_global, down_moment,
    up_new, up_mom, down_new, down_mom, out_ref, weights, moment,
):
    groups, _, width = up_global.shape
    up_blocks = width // LANES
    down_blocks = down_global.shape[1] // LANES
    places = [
        (j, (g, slice(0, 1), slice(s * LANES, (s + 1) * LANES))) for j, g, s in up_slots(groups, up_blocks)
    ]
    down_places = [
        (groups * up_blocks + t, (slice(0, 1), slice(t * LANES, (t + 1) * LANES))) for t in range(down_blocks)
    ]
    for j, at in places:
        weights[j : j + 1, :] = up_global[at]
        moment[j : j + 1, :] = up_moment[at]
    for j, at in down_places:
        weights[j : j + 1, :] = down_global[at]
        moment[j : j + 1, :] = down_moment[at]
    total = jnp.sum(recv[...].astype(jnp.float32), axis=0)
    mean = total / recv.shape[0]
    moment_new = nesterov * moment[...] + mean
    weights_new = weights[...] - outer_rate * (mean + nesterov * moment_new)
    shared = weights_new.astype(jnp.bfloat16)
    for r in range(out_ref.shape[0]):
        out_ref[r] = shared
    weights[...] = weights_new
    moment[...] = moment_new
    for j, at in places:
        up_new[at] = weights[j : j + 1, :]
        up_mom[at] = moment[j : j + 1, :]
    for j, at in down_places:
        down_new[at] = weights[j : j + 1, :]
        down_mom[at] = moment[j : j + 1, :]


def merge_kernel(recv, up_local, down_local, up_merged, down_merged, shared):
    groups, rows, width = up_local.shape
    up_blocks = width // LANES
    down_blocks = down_local.shape[1] // LANES
    slots = recv.shape[1]
    for r in range(rows):
        shared[r * slots : (r + 1) * slots, :] = recv[r].astype(jnp.float32)

    def merged(local, j):
        theirs = shared[pl.ds(j, rows, stride=slots), :]
        return (mixing * local.astype(jnp.float32) + (1.0 - mixing) * theirs).astype(jnp.bfloat16)

    for j, g, s in up_slots(groups, up_blocks):
        at = (g, slice(None), slice(s * LANES, (s + 1) * LANES))
        up_merged[at] = merged(up_local[at], j)
    for t in range(down_blocks):
        at = (slice(None), slice(t * LANES, (t + 1) * LANES))
        down_merged[at] = merged(down_local[at], groups * up_blocks + t)


def per_device(
    code_table,
    up_codes,
    up_exps,
    up_global,
    up_moment,
    up_local,
    down_codes,
    down_exps,
    down_global,
    down_moment,
    down_local,
):
    _, groups, rows, width = up_codes.shape
    depth = down_codes.shape[-1]
    slots = (groups * width + depth) // LANES
    chunk = jax.ShapeDtypeStruct((rows, slots, LANES), jnp.bfloat16)
    sds = jax.ShapeDtypeStruct
    decoded = pl.pallas_call(
        decode_kernel,
        out_shape=chunk,
        in_specs=[SMEM, VMEM, VMEM, VMEM, VMEM],
        out_specs=VMEM,
        scratch_shapes=[pltpu.VMEM((rows * slots, LANES), jnp.int32), pltpu.VMEM((slots, rows), jnp.int32)],
    )(
        code_table,
        up_codes[0],
        jnp.transpose(up_exps[0], (2, 0, 1)),
        down_codes[0],
        jnp.transpose(down_exps[0], (1, 0)),
    )
    recv = lax.all_to_all(decoded, "replica", split_axis=0, concat_axis=0, tiled=True)
    up_new, up_mom, down_new, down_mom, shared = pl.pallas_call(
        advance_kernel,
        out_shape=(
            sds(up_global.shape, jnp.float32),
            sds(up_global.shape, jnp.float32),
            sds(down_global.shape, jnp.float32),
            sds(down_global.shape, jnp.float32),
            chunk,
        ),
        in_specs=[VMEM] * 5,
        out_specs=(VMEM,) * 5,
        scratch_shapes=[pltpu.VMEM((slots, LANES), jnp.float32), pltpu.VMEM((slots, LANES), jnp.float32)],
    )(recv, up_global, up_moment, down_global, down_moment)
    spread = lax.all_to_all(shared, "replica", split_axis=0, concat_axis=0, tiled=True)
    up_merged, down_merged = pl.pallas_call(
        merge_kernel,
        out_shape=(sds(up_local.shape[1:], jnp.bfloat16), sds(down_local.shape[1:], jnp.bfloat16)),
        in_specs=[VMEM] * 3,
        out_specs=(VMEM,) * 2,
        scratch_shapes=[pltpu.VMEM((rows * slots, LANES), jnp.float32)],
    )(spread, up_local[0], down_local[0])
    return (up_new, up_mom, up_merged[None], down_new, down_mom, down_merged[None])


def solution(mesh):
    in_specs = (
        P(),
        P("replica", None, None, "mp"),
        P("replica", None, None, "mp"),
        P(None, "replica", "mp"),
        P(None, "replica", "mp"),
        P("replica", None, None, "mp"),
        P("replica", None, "mp"),
        P("replica", None, "mp"),
        P("replica", "mp"),
        P("replica", "mp"),
        P("replica", None, "mp"),
    )
    out_specs = (
        P(None, "replica", "mp"),
        P(None, "replica", "mp"),
        P("replica", None, None, "mp"),
        P("replica", "mp"),
        P("replica", "mp"),
        P("replica", None, "mp"),
    )
    return jax.shard_map(
        per_device, mesh=mesh, in_specs=in_specs, out_specs=out_specs, check_vma=False
    )
```

```python
import jax
import jax.numpy as jnp
from jax import lax
from jax.experimental import pallas as pl
from jax.experimental.pallas import tpu as pltpu
from jax.sharding import PartitionSpec as P

LANES = 128
LOW_EXP = -8

outer_rate = 0.7
nesterov = 0.9
mixing = 0.5

VMEM = pl.BlockSpec(memory_space=pltpu.VMEM)
HBM = pl.BlockSpec(memory_space=pltpu.HBM)


PARAMS = pltpu.CompilerParams(vmem_limit_bytes=4 * 1024 * 1024)


def up_slots(groups, blocks):
    return [(s * groups + g, g, s) for s in range(blocks) for g in range(groups)]


def decode_kernel(
    table_hbm, up_codes_hbm, up_exps_hbm, down_codes_hbm, down_exps_hbm, out_ref,
    table_ref, up_codes, up_exps, down_codes, down_exps, codes_by_row, exps_by_slot, sems,
):
    copies = [
        pltpu.make_async_copy(source, target, sems.at[i])
        for i, (source, target) in enumerate(
            [
                (table_hbm, table_ref),
                (up_exps_hbm, up_exps),
                (down_exps_hbm, down_exps),
                (down_codes_hbm, down_codes),
                (up_codes_hbm, up_codes),
            ]
        )
    ]
    for copy in copies:
        copy.start()
    groups, rows, width = up_codes.shape
    up_blocks = width // LANES
    down_blocks = down_codes.shape[1] // LANES
    slots = groups * up_blocks + down_blocks
    copies[0].wait()
    lane = lax.broadcasted_iota(jnp.int32, (slots, LANES), 1)
    table = jnp.zeros((slots, LANES), jnp.int32)
    for level in range(16):
        table = jnp.where(lane == level, table_ref[level], table)
    table = table.astype(jnp.float32)
    for copy in copies[1:4]:
        copy.wait()
    for j, g, s in up_slots(groups, up_blocks):
        exps_by_slot[j : j + 1, :] = up_exps[s, g : g + 1, :]
    for t in range(down_blocks):
        j = groups * up_blocks + t
        codes_by_row[pl.ds(j, rows, stride=slots), :] = down_codes[:, t * LANES : (t + 1) * LANES]
        exps_by_slot[j : j + 1, :] = down_exps[t : t + 1, :]
    scales = jnp.left_shift(1, exps_by_slot[...] - LOW_EXP).astype(jnp.float32) * 2.0**LOW_EXP
    copies[4].wait()
    for j, g, s in up_slots(groups, up_blocks):
        codes_by_row[pl.ds(j, rows, stride=slots), :] = up_codes[g, :, s * LANES : (s + 1) * LANES]
    for r in range(rows):
        codes = codes_by_row[r * slots : (r + 1) * slots, :]
        values = jnp.take_along_axis(table, codes, axis=1)
        out_ref[r] = (values * scales[:, r : r + 1]).astype(jnp.bfloat16)


def chip_sum_kernel(recv, up_global, up_moment, down_global, down_moment, out_ref):
    groups, _, width = up_global.shape
    up_blocks = width // LANES
    for k in range(2):
        total = recv[k].astype(jnp.float32)
        for q in range(1, recv.shape[0] // 2):
            total = total + recv[2 * q + k].astype(jnp.float32)
        out_ref[k] = total
    for j, g, s in up_slots(groups, up_blocks):
        out_ref[2, j : j + 1, :] = up_global[g, :, s * LANES : (s + 1) * LANES]
        out_ref[3, j : j + 1, :] = up_moment[g, :, s * LANES : (s + 1) * LANES]
    for t in range(down_global.shape[1] // LANES):
        j = groups * up_blocks + t
        out_ref[2, j : j + 1, :] = down_global[:, t * LANES : (t + 1) * LANES]
        out_ref[3, j : j + 1, :] = down_moment[:, t * LANES : (t + 1) * LANES]


def advance_kernel(both, up_new, up_mom, down_new, down_mom, out_ref, weights, moment):
    core = lax.rem(lax.axis_index("replica"), 2)
    replicas = out_ref.shape[0]
    for k in range(2):
        mean = (both[k] + both[4 + k]) / replicas
        moment_new = nesterov * both[4 * k + 3] + mean
        weights_new = both[4 * k + 2] - outer_rate * (mean + nesterov * moment_new)
        shared = weights_new.astype(jnp.bfloat16)
        for q in range(replicas // 2):
            out_ref[2 * q + k] = shared
        weights[k] = weights_new
        moment[k] = moment_new
    groups, _, width = up_new.shape
    up_blocks = width // LANES
    for j, g, s in up_slots(groups, up_blocks):
        up_new[g, :, s * LANES : (s + 1) * LANES] = weights[core, j : j + 1, :]
        up_mom[g, :, s * LANES : (s + 1) * LANES] = moment[core, j : j + 1, :]
    for t in range(down_new.shape[1] // LANES):
        j = groups * up_blocks + t
        down_new[:, t * LANES : (t + 1) * LANES] = weights[core, j : j + 1, :]
        down_mom[:, t * LANES : (t + 1) * LANES] = moment[core, j : j + 1, :]


def merge_kernel(recv, up_local, down_local, up_merged, down_merged, shared):
    groups, rows, width = up_local.shape
    up_blocks = width // LANES
    down_blocks = down_local.shape[1] // LANES
    slots = recv.shape[1]
    for r in range(rows):
        shared[r * slots : (r + 1) * slots, :] = recv[r].astype(jnp.float32)

    def merged(local, j):
        theirs = shared[pl.ds(j, rows, stride=slots), :]
        return (mixing * local.astype(jnp.float32) + (1.0 - mixing) * theirs).astype(jnp.bfloat16)

    for j, g, s in up_slots(groups, up_blocks):
        at = (g, slice(None), slice(s * LANES, (s + 1) * LANES))
        up_merged[at] = merged(up_local[at], j)
    for t in range(down_blocks):
        at = (slice(None), slice(t * LANES, (t + 1) * LANES))
        down_merged[at] = merged(down_local[at], groups * up_blocks + t)


def per_device(
    code_table,
    up_codes,
    up_exps,
    up_global,
    up_moment,
    up_local,
    down_codes,
    down_exps,
    down_global,
    down_moment,
    down_local,
):
    _, groups, rows, width = up_codes.shape
    depth = down_codes.shape[-1]
    slots = (groups * width + depth) // LANES
    chips = rows // 2
    pairs = [[2 * q, 2 * q + 1] for q in range(chips)]
    sides = [[2 * q + c for q in range(chips)] for c in range(2)]
    sds = jax.ShapeDtypeStruct
    chunks = sds((rows, slots, LANES), jnp.bfloat16)
    up_exps = jnp.transpose(up_exps[0], (2, 0, 1))
    down_exps = jnp.transpose(down_exps[0], (1, 0))
    streamed = (code_table, up_codes[0], up_exps, down_codes[0], down_exps)
    decoded = pl.pallas_call(
        decode_kernel,
        compiler_params=PARAMS,
        out_shape=chunks,
        in_specs=[HBM] * 5,
        out_specs=VMEM,
        scratch_shapes=[
            pltpu.SMEM(code_table.shape, jnp.int32),
            pltpu.VMEM(up_codes.shape[1:], jnp.int32),
            pltpu.VMEM(up_exps.shape, jnp.int32),
            pltpu.VMEM(down_codes.shape[1:], jnp.int32),
            pltpu.VMEM(down_exps.shape, jnp.int32),
            pltpu.VMEM((rows * slots, LANES), jnp.int32),
            pltpu.VMEM((slots, rows), jnp.int32),
            pltpu.SemaphoreType.DMA((5,)),
        ],
    )(*[pltpu.with_memory_space_constraint(x, pltpu.HBM) for x in streamed])
    recv = lax.all_to_all(decoded, "replica", split_axis=0, concat_axis=0, axis_index_groups=sides, tiled=True)
    mine = pl.pallas_call(
        chip_sum_kernel,
        compiler_params=PARAMS,
        out_shape=sds((4, slots, LANES), jnp.float32),
        in_specs=[VMEM] * 5,
        out_specs=VMEM,
    )(recv, up_global, up_moment, down_global, down_moment)
    both = lax.all_gather(mine, "replica", axis=0, axis_index_groups=pairs, tiled=True)
    up_new, up_mom, down_new, down_mom, shared = pl.pallas_call(
        advance_kernel,
        compiler_params=PARAMS,
        out_shape=(
            sds(up_global.shape, jnp.float32),
            sds(up_global.shape, jnp.float32),
            sds(down_global.shape, jnp.float32),
            sds(down_global.shape, jnp.float32),
            chunks,
        ),
        in_specs=[VMEM],
        out_specs=(VMEM,) * 5,
        scratch_shapes=[pltpu.VMEM((2, slots, LANES), jnp.float32), pltpu.VMEM((2, slots, LANES), jnp.float32)],
    )(both)
    spread = lax.all_to_all(shared, "replica", split_axis=0, concat_axis=0, axis_index_groups=sides, tiled=True)
    up_merged, down_merged = pl.pallas_call(
        merge_kernel,
        compiler_params=PARAMS,
        out_shape=(sds(up_local.shape[1:], jnp.bfloat16), sds(down_local.shape[1:], jnp.bfloat16)),
        in_specs=[VMEM] * 3,
        out_specs=(VMEM,) * 2,
        scratch_shapes=[pltpu.VMEM((rows * slots, LANES), jnp.float32)],
    )(spread, up_local[0], down_local[0])
    return (up_new, up_mom, up_merged[None], down_new, down_mom, down_merged[None])


def solution(mesh):
    in_specs = (
        P(),
        P("replica", None, None, "mp"),
        P("replica", None, None, "mp"),
        P(None, "replica", "mp"),
        P(None, "replica", "mp"),
        P("replica", None, None, "mp"),
        P("replica", None, "mp"),
        P("replica", None, "mp"),
        P("replica", "mp"),
        P("replica", "mp"),
        P("replica", None, "mp"),
    )
    out_specs = (
        P(None, "replica", "mp"),
        P(None, "replica", "mp"),
        P("replica", None, None, "mp"),
        P("replica", "mp"),
        P("replica", "mp"),
        P("replica", None, "mp"),
    )
    return jax.shard_map(
        per_device, mesh=mesh, in_specs=in_specs, out_specs=out_specs, check_vma=False
    )
```

```python
import jax
import jax.numpy as jnp
from jax import lax
from jax.experimental import pallas as pl
from jax.experimental.pallas import tpu as pltpu
from jax.sharding import PartitionSpec as P

LANES = 128
LOW_EXP = -8

outer_rate = 0.7
nesterov = 0.9
mixing = 0.5

VMEM = pl.BlockSpec(memory_space=pltpu.VMEM)
HBM = pl.BlockSpec(memory_space=pltpu.HBM)


PARAMS = pltpu.CompilerParams(vmem_limit_bytes=4 * 1024 * 1024)


def up_slots(groups, blocks):
    return [(s * groups + g, g, s) for s in range(blocks) for g in range(groups)]


def decode_kernel(
    table_hbm, up_codes_hbm, up_exps_hbm, down_codes_hbm, down_exps_hbm, out_ref,
    table_ref, up_codes, up_exps, down_codes, down_exps, codes_by_row, exps_by_slot, sems,
):
    copies = [
        pltpu.make_async_copy(source, target, sems.at[i])
        for i, (source, target) in enumerate(
            [
                (table_hbm, table_ref),
                (up_exps_hbm, up_exps),
                (down_exps_hbm, down_exps),
                (down_codes_hbm, down_codes),
                (up_codes_hbm, up_codes),
            ]
        )
    ]
    for copy in copies:
        copy.start()
    groups, rows, width = up_codes.shape
    up_blocks = width // LANES
    down_blocks = down_codes.shape[1] // LANES
    slots = groups * up_blocks + down_blocks
    copies[0].wait()
    lane = lax.broadcasted_iota(jnp.int32, (slots, LANES), 1)
    table = jnp.zeros((slots, LANES), jnp.int32)
    for level in range(16):
        table = jnp.where(lane == level, table_ref[level], table)
    table = table.astype(jnp.float32)
    for copy in copies[1:4]:
        copy.wait()
    for j, g, s in up_slots(groups, up_blocks):
        exps_by_slot[j : j + 1, :] = up_exps[s, g : g + 1, :]
    for t in range(down_blocks):
        j = groups * up_blocks + t
        codes_by_row[pl.ds(j, rows, stride=slots), :] = down_codes[:, t * LANES : (t + 1) * LANES]
        exps_by_slot[j : j + 1, :] = down_exps[t : t + 1, :]
    scales = jnp.left_shift(1, exps_by_slot[...] - LOW_EXP).astype(jnp.float32) * 2.0**LOW_EXP
    copies[4].wait()
    for j, g, s in up_slots(groups, up_blocks):
        codes_by_row[pl.ds(j, rows, stride=slots), :] = up_codes[g, :, s * LANES : (s + 1) * LANES]
    for r in range(rows):
        codes = codes_by_row[r * slots : (r + 1) * slots, :]
        values = jnp.take_along_axis(table, codes, axis=1)
        out_ref[r] = (values * scales[:, r : r + 1]).astype(jnp.bfloat16)


def chip_sum_kernel(recv, up_global, up_moment, down_global, down_moment, out_ref):
    groups, _, width = up_global.shape
    up_blocks = width // LANES
    for k in range(2):
        total = recv[k].astype(jnp.float32)
        for q in range(1, recv.shape[0] // 2):
            total = total + recv[2 * q + k].astype(jnp.float32)
        out_ref[k] = total
    for j, g, s in up_slots(groups, up_blocks):
        out_ref[2, j : j + 1, :] = up_global[g, :, s * LANES : (s + 1) * LANES]
        out_ref[3, j : j + 1, :] = up_moment[g, :, s * LANES : (s + 1) * LANES]
    for t in range(down_global.shape[1] // LANES):
        j = groups * up_blocks + t
        out_ref[2, j : j + 1, :] = down_global[:, t * LANES : (t + 1) * LANES]
        out_ref[3, j : j + 1, :] = down_moment[:, t * LANES : (t + 1) * LANES]


def advance_kernel(both, out_ref, state, rows_new):
    core = lax.rem(lax.axis_index("replica"), 2)
    replicas = out_ref.shape[0]
    for k in range(2):
        mean = (both[k] + both[4 + k]) / replicas
        moment_new = nesterov * both[4 * k + 3] + mean
        weights_new = both[4 * k + 2] - outer_rate * (mean + nesterov * moment_new)
        shared = weights_new.astype(jnp.bfloat16)
        for q in range(replicas // 2):
            out_ref[2 * q + k] = shared
        rows_new[k, 0] = weights_new
        rows_new[k, 1] = moment_new
    state[...] = rows_new[core]


def merge_kernel(
    recv, up_local, down_local, state, up_merged, down_merged, up_new, up_mom, down_new, down_mom, shared
):
    groups, rows, width = up_local.shape
    up_blocks = width // LANES
    down_blocks = down_local.shape[1] // LANES
    slots = recv.shape[1]
    for r in range(rows):
        shared[r * slots : (r + 1) * slots, :] = recv[r].astype(jnp.float32)

    def merged(local, j):
        theirs = shared[pl.ds(j, rows, stride=slots), :]
        return (mixing * local.astype(jnp.float32) + (1.0 - mixing) * theirs).astype(jnp.bfloat16)

    for j, g, s in up_slots(groups, up_blocks):
        lanes = slice(s * LANES, (s + 1) * LANES)
        up_merged[g, :, lanes] = merged(up_local[g, :, lanes], j)
        up_new[g, :, lanes] = state[0, j : j + 1, :]
        up_mom[g, :, lanes] = state[1, j : j + 1, :]
    for t in range(down_blocks):
        j = groups * up_blocks + t
        lanes = slice(t * LANES, (t + 1) * LANES)
        down_merged[:, lanes] = merged(down_local[:, lanes], j)
        down_new[:, lanes] = state[0, j : j + 1, :]
        down_mom[:, lanes] = state[1, j : j + 1, :]


def per_device(
    code_table,
    up_codes,
    up_exps,
    up_global,
    up_moment,
    up_local,
    down_codes,
    down_exps,
    down_global,
    down_moment,
    down_local,
):
    _, groups, rows, width = up_codes.shape
    depth = down_codes.shape[-1]
    slots = (groups * width + depth) // LANES
    chips = rows // 2
    pairs = [[2 * q, 2 * q + 1] for q in range(chips)]
    sides = [[2 * q + c for q in range(chips)] for c in range(2)]
    sds = jax.ShapeDtypeStruct
    chunks = sds((rows, slots, LANES), jnp.bfloat16)
    up_exps = jnp.transpose(up_exps[0], (2, 0, 1))
    down_exps = jnp.transpose(down_exps[0], (1, 0))
    streamed = (code_table, up_codes[0], up_exps, down_codes[0], down_exps)
    decoded = pl.pallas_call(
        decode_kernel,
        compiler_params=PARAMS,
        out_shape=chunks,
        in_specs=[HBM] * 5,
        out_specs=VMEM,
        scratch_shapes=[
            pltpu.SMEM(code_table.shape, jnp.int32),
            pltpu.VMEM(up_codes.shape[1:], jnp.int32),
            pltpu.VMEM(up_exps.shape, jnp.int32),
            pltpu.VMEM(down_codes.shape[1:], jnp.int32),
            pltpu.VMEM(down_exps.shape, jnp.int32),
            pltpu.VMEM((rows * slots, LANES), jnp.int32),
            pltpu.VMEM((slots, rows), jnp.int32),
            pltpu.SemaphoreType.DMA((5,)),
        ],
    )(*[pltpu.with_memory_space_constraint(x, pltpu.HBM) for x in streamed])
    recv = lax.all_to_all(decoded, "replica", split_axis=0, concat_axis=0, axis_index_groups=sides, tiled=True)
    mine = pl.pallas_call(
        chip_sum_kernel,
        compiler_params=PARAMS,
        out_shape=sds((4, slots, LANES), jnp.float32),
        in_specs=[VMEM] * 5,
        out_specs=VMEM,
    )(recv, up_global, up_moment, down_global, down_moment)
    both = lax.all_gather(mine, "replica", axis=0, axis_index_groups=pairs, tiled=True)
    shared, state = pl.pallas_call(
        advance_kernel,
        compiler_params=PARAMS,
        out_shape=(chunks, sds((2, slots, LANES), jnp.float32)),
        in_specs=[VMEM],
        out_specs=(VMEM,) * 2,
        scratch_shapes=[pltpu.VMEM((2, 2, slots, LANES), jnp.float32)],
    )(both)
    spread = lax.all_to_all(shared, "replica", split_axis=0, concat_axis=0, axis_index_groups=sides, tiled=True)
    up_merged, down_merged, up_new, up_mom, down_new, down_mom = pl.pallas_call(
        merge_kernel,
        compiler_params=PARAMS,
        out_shape=(
            sds(up_local.shape[1:], jnp.bfloat16),
            sds(down_local.shape[1:], jnp.bfloat16),
            sds(up_global.shape, jnp.float32),
            sds(up_global.shape, jnp.float32),
            sds(down_global.shape, jnp.float32),
            sds(down_global.shape, jnp.float32),
        ),
        in_specs=[VMEM] * 4,
        out_specs=(VMEM,) * 6,
        scratch_shapes=[pltpu.VMEM((rows * slots, LANES), jnp.float32)],
    )(spread, up_local[0], down_local[0], state)
    return (up_new, up_mom, up_merged[None], down_new, down_mom, down_merged[None])


def solution(mesh):
    in_specs = (
        P(),
        P("replica", None, None, "mp"),
        P("replica", None, None, "mp"),
        P(None, "replica", "mp"),
        P(None, "replica", "mp"),
        P("replica", None, None, "mp"),
        P("replica", None, "mp"),
        P("replica", None, "mp"),
        P("replica", "mp"),
        P("replica", "mp"),
        P("replica", None, "mp"),
    )
    out_specs = (
        P(None, "replica", "mp"),
        P(None, "replica", "mp"),
        P("replica", None, None, "mp"),
        P("replica", "mp"),
        P("replica", "mp"),
        P("replica", None, "mp"),
    )
    return jax.shard_map(
        per_device, mesh=mesh, in_specs=in_specs, out_specs=out_specs, check_vma=False
    )
```

```python
import jax
import jax.numpy as jnp
from jax import lax
from jax.experimental import pallas as pl
from jax.experimental.pallas import tpu as pltpu
from jax.sharding import PartitionSpec as P

LANES = 128
LOW_EXP = -8

outer_rate = 0.7
nesterov = 0.9
mixing = 0.5

VMEM = pl.BlockSpec(memory_space=pltpu.VMEM)
HBM = pl.BlockSpec(memory_space=pltpu.HBM)


PARAMS = pltpu.CompilerParams(vmem_limit_bytes=4 * 1024 * 1024)


def up_slots(groups, blocks):
    return [(s * groups + g, g, s) for s in range(blocks) for g in range(groups)]


def pieces_of(x):
    high = x.astype(jnp.bfloat16)
    rest = x - high.astype(jnp.float32)
    middle = rest.astype(jnp.bfloat16)
    low = (rest - middle.astype(jnp.float32)).astype(jnp.bfloat16)
    return [high, middle, low]


def sum_of(ref, first):
    high, middle, low = [ref[first + i].astype(jnp.float32) for i in range(3)]
    return (high + middle) + low


def decode_kernel(
    table_hbm, up_exps_hbm, down_exps_hbm, up_global_hbm, up_moment_hbm, down_global_hbm, down_moment_hbm,
    down_codes_hbm, up_codes_hbm, out_ref,
    table_ref, up_exps, down_exps, up_global, up_moment, down_global, down_moment, down_codes, up_codes,
    codes_by_row, exps_by_slot, owned, sems,
):
    sources = [
        table_hbm, up_exps_hbm, down_exps_hbm, up_global_hbm, up_moment_hbm, down_global_hbm, down_moment_hbm,
        down_codes_hbm, up_codes_hbm,
    ]
    targets = [
        table_ref, up_exps, down_exps, up_global, up_moment, down_global, down_moment, down_codes, up_codes,
    ]
    copies = [pltpu.make_async_copy(a, b, sems.at[i]) for i, (a, b) in enumerate(zip(sources, targets))]
    for copy in reversed(copies):
        copy.start()
    groups, rows, width = up_codes.shape
    up_blocks = width // LANES
    down_blocks = down_codes.shape[1] // LANES
    slots = groups * up_blocks + down_blocks
    copies[0].wait()
    lane = lax.broadcasted_iota(jnp.int32, (slots, LANES), 1)
    table = jnp.zeros((slots, LANES), jnp.int32)
    for level in range(16):
        table = jnp.where(lane == level, table_ref[level], table)
    table = table.astype(jnp.float32)
    for copy in copies[1:-1]:
        copy.wait()
    for j, g, s in up_slots(groups, up_blocks):
        lanes = slice(s * LANES, (s + 1) * LANES)
        exps_by_slot[j : j + 1, :] = up_exps[s, g : g + 1, :]
        owned[0, j : j + 1, :] = up_global[g, :, lanes]
        owned[1, j : j + 1, :] = up_moment[g, :, lanes]
    for t in range(down_blocks):
        j = groups * up_blocks + t
        lanes = slice(t * LANES, (t + 1) * LANES)
        codes_by_row[pl.ds(j, rows, stride=slots), :] = down_codes[:, lanes]
        exps_by_slot[j : j + 1, :] = down_exps[t : t + 1, :]
        owned[0, j : j + 1, :] = down_global[:, lanes]
        owned[1, j : j + 1, :] = down_moment[:, lanes]
    for k in range(2):
        for i, piece in enumerate(pieces_of(owned[k])):
            out_ref[rows + 3 * k + i] = piece
    scales = jnp.left_shift(1, exps_by_slot[...] - LOW_EXP).astype(jnp.float32) * 2.0**LOW_EXP
    copies[-1].wait()
    for j, g, s in up_slots(groups, up_blocks):
        codes_by_row[pl.ds(j, rows, stride=slots), :] = up_codes[g, :, s * LANES : (s + 1) * LANES]
    for r in range(rows):
        codes = codes_by_row[r * slots : (r + 1) * slots, :]
        values = jnp.take_along_axis(table, codes, axis=1)
        out_ref[r] = (values * scales[:, r : r + 1]).astype(jnp.bfloat16)


def pair_kernel(both, out_ref):
    rows = out_ref.shape[0]
    step = both.shape[0] // 2
    for r in range(rows):
        total = both[r].astype(jnp.float32) + both[step + r].astype(jnp.float32)
        out_ref[r] = (total * 2.0**-LOW_EXP).astype(jnp.int32).astype(jnp.int16)


def advanced(mean, weights, moment):
    moment_new = nesterov * moment + mean
    return weights - outer_rate * (mean + nesterov * moment_new), moment_new


def advance_kernel(recv, both, out_ref, totals):
    replicas = out_ref.shape[0]
    step = both.shape[0] // 2
    for k in range(2):
        total = recv[k].astype(jnp.int32)
        for q in range(1, replicas // 2):
            total = total + recv[2 * q + k].astype(jnp.int32)
        total = total.astype(jnp.float32)
        first = step * k + replicas
        mean = total * (2.0**LOW_EXP / replicas)
        weights_new, _ = advanced(mean, sum_of(both, first), sum_of(both, first + 3))
        shared = weights_new.astype(jnp.bfloat16)
        for q in range(replicas // 2):
            out_ref[2 * q + k] = shared
        high = total.astype(jnp.bfloat16)
        totals[2 * k] = high
        totals[2 * k + 1] = (total - high.astype(jnp.float32)).astype(jnp.bfloat16)


def join_kernel(spread, totals, out_ref):
    rows = spread.shape[0]
    out_ref[0:rows] = spread[...]
    out_ref[rows:] = totals[...]


def merge_kernel(
    both, decoded, up_local, down_local, up_merged, down_merged, up_new, up_mom, down_new, down_mom, shared, state
):
    groups, rows, width = up_local.shape
    up_blocks = width // LANES
    down_blocks = down_local.shape[1] // LANES
    step, slots = both.shape[0] // 2, both.shape[1]
    core = lax.rem(lax.axis_index("replica"), 2)
    first = step + rows + 2 * core
    total = both[first].astype(jnp.float32) + both[first + 1].astype(jnp.float32)
    mean = total * (2.0**LOW_EXP / rows)
    state[0], state[1] = advanced(mean, sum_of(decoded, rows), sum_of(decoded, rows + 3))
    for r in range(rows):
        shared[r * slots : (r + 1) * slots, :] = both[step + r].astype(jnp.float32)

    def merged(local, j):
        theirs = shared[pl.ds(j, rows, stride=slots), :]
        return (mixing * local.astype(jnp.float32) + (1.0 - mixing) * theirs).astype(jnp.bfloat16)

    for j, g, s in up_slots(groups, up_blocks):
        lanes = slice(s * LANES, (s + 1) * LANES)
        up_merged[g, :, lanes] = merged(up_local[g, :, lanes], j)
        up_new[g, :, lanes] = state[0, j : j + 1, :]
        up_mom[g, :, lanes] = state[1, j : j + 1, :]
    for t in range(down_blocks):
        j = groups * up_blocks + t
        lanes = slice(t * LANES, (t + 1) * LANES)
        down_merged[:, lanes] = merged(down_local[:, lanes], j)
        down_new[:, lanes] = state[0, j : j + 1, :]
        down_mom[:, lanes] = state[1, j : j + 1, :]


def per_device(
    code_table,
    up_codes,
    up_exps,
    up_global,
    up_moment,
    up_local,
    down_codes,
    down_exps,
    down_global,
    down_moment,
    down_local,
):
    _, groups, rows, width = up_codes.shape
    depth = down_codes.shape[-1]
    slots = (groups * width + depth) // LANES
    chips = rows // 2
    pairs = [[2 * q, 2 * q + 1] for q in range(chips)]
    sides = [[2 * q + c for q in range(chips)] for c in range(2)]
    core = lax.rem(lax.axis_index("replica"), 2)
    sds = jax.ShapeDtypeStruct

    def across(x):
        return lax.cond(
            core == 1,
            lambda v: lax.all_to_all(v, "replica", split_axis=0, concat_axis=0, axis_index_groups=sides, tiled=True),
            lambda v: v,
            x,
        )

    streamed = (
        code_table,
        jnp.transpose(up_exps[0], (2, 0, 1)),
        jnp.transpose(down_exps[0], (1, 0)),
        up_global,
        up_moment,
        down_global,
        down_moment,
        down_codes[0],
        up_codes[0],
    )
    decoded = pl.pallas_call(
        decode_kernel,
        compiler_params=PARAMS,
        out_shape=sds((rows + 6, slots, LANES), jnp.bfloat16),
        in_specs=[HBM] * len(streamed),
        out_specs=VMEM,
        scratch_shapes=[
            pltpu.SMEM(code_table.shape, jnp.int32),
            *[pltpu.VMEM(x.shape, x.dtype) for x in streamed[1:]],
            pltpu.VMEM((rows * slots, LANES), jnp.int32),
            pltpu.VMEM((slots, rows), jnp.int32),
            pltpu.VMEM((2, slots, LANES), jnp.float32),
            pltpu.SemaphoreType.DMA((len(streamed),)),
        ],
    )(*[pltpu.with_memory_space_constraint(x, pltpu.HBM) for x in streamed])
    both = lax.all_gather(decoded, "replica", axis=0, axis_index_groups=pairs, tiled=True)
    sums = pl.pallas_call(
        pair_kernel,
        compiler_params=PARAMS,
        out_shape=sds((rows, slots, LANES), jnp.int16),
        in_specs=[VMEM],
        out_specs=VMEM,
    )(both)
    recv = across(sums)
    shared, totals = pl.pallas_call(
        advance_kernel,
        compiler_params=PARAMS,
        out_shape=(sds((rows, slots, LANES), jnp.bfloat16), sds((4, slots, LANES), jnp.bfloat16)),
        in_specs=[VMEM] * 2,
        out_specs=(VMEM,) * 2,
    )(recv, both)
    spread = across(shared)
    joined = pl.pallas_call(
        join_kernel,
        compiler_params=PARAMS,
        out_shape=sds((rows + 4, slots, LANES), jnp.bfloat16),
        in_specs=[VMEM] * 2,
        out_specs=VMEM,
    )(spread, totals)
    final = lax.all_gather(joined, "replica", axis=0, axis_index_groups=pairs, tiled=True)
    up_merged, down_merged, up_new, up_mom, down_new, down_mom = pl.pallas_call(
        merge_kernel,
        compiler_params=PARAMS,
        out_shape=(
            sds(up_local.shape[1:], jnp.bfloat16),
            sds(down_local.shape[1:], jnp.bfloat16),
            sds(up_global.shape, jnp.float32),
            sds(up_global.shape, jnp.float32),
            sds(down_global.shape, jnp.float32),
            sds(down_global.shape, jnp.float32),
        ),
        in_specs=[VMEM] * 4,
        out_specs=(VMEM,) * 6,
        scratch_shapes=[pltpu.VMEM((rows * slots, LANES), jnp.float32), pltpu.VMEM((2, slots, LANES), jnp.float32)],
    )(final, decoded, up_local[0], down_local[0])
    return (up_new, up_mom, up_merged[None], down_new, down_mom, down_merged[None])


def solution(mesh):
    in_specs = (
        P(),
        P("replica", None, None, "mp"),
        P("replica", None, None, "mp"),
        P(None, "replica", "mp"),
        P(None, "replica", "mp"),
        P("replica", None, None, "mp"),
        P("replica", None, "mp"),
        P("replica", None, "mp"),
        P("replica", "mp"),
        P("replica", "mp"),
        P("replica", None, "mp"),
    )
    out_specs = (
        P(None, "replica", "mp"),
        P(None, "replica", "mp"),
        P("replica", None, None, "mp"),
        P("replica", "mp"),
        P("replica", "mp"),
        P("replica", None, "mp"),
    )
    return jax.shard_map(
        per_device, mesh=mesh, in_specs=in_specs, out_specs=out_specs, check_vma=False
    )
```

```python
import jax
import jax.numpy as jnp
from jax import lax
from jax.experimental import pallas as pl
from jax.experimental.pallas import tpu as pltpu
from jax.sharding import PartitionSpec as P

LANES = 128
LOW_EXP = -8

outer_rate = 0.7
nesterov = 0.9
mixing = 0.5

VMEM = pl.BlockSpec(memory_space=pltpu.VMEM)
HBM = pl.BlockSpec(memory_space=pltpu.HBM)


PARAMS = pltpu.CompilerParams(vmem_limit_bytes=4 * 1024 * 1024)


def up_slots(groups, blocks):
    return [(s * groups + g, g, s) for s in range(blocks) for g in range(groups)]


def decode_kernel(
    table_hbm, up_codes_hbm, up_exps_hbm, down_codes_hbm, down_exps_hbm, out_ref,
    table_ref, up_codes, up_exps, down_codes, down_exps, codes_by_row, exps_by_slot, sems,
):
    copies = [
        pltpu.make_async_copy(source, target, sems.at[i])
        for i, (source, target) in enumerate(
            [
                (table_hbm, table_ref),
                (up_exps_hbm, up_exps),
                (down_exps_hbm, down_exps),
                (down_codes_hbm, down_codes),
                (up_codes_hbm, up_codes),
            ]
        )
    ]
    for copy in reversed(copies):
        copy.start()
    groups, rows, width = up_codes.shape
    up_blocks = width // LANES
    down_blocks = down_codes.shape[1] // LANES
    slots = groups * up_blocks + down_blocks
    copies[0].wait()
    table = [table_ref[level].astype(jnp.float32) for level in range(16)]
    for copy in copies[1:4]:
        copy.wait()
    for j, g, s in up_slots(groups, up_blocks):
        exps_by_slot[j : j + 1, :] = up_exps[s, g : g + 1, :]
    for t in range(down_blocks):
        j = groups * up_blocks + t
        codes_by_row[pl.ds(j, rows, stride=slots), :] = down_codes[:, t * LANES : (t + 1) * LANES]
        exps_by_slot[j : j + 1, :] = down_exps[t : t + 1, :]
    scales = jnp.left_shift(1, exps_by_slot[...] - LOW_EXP).astype(jnp.float32) * 2.0**LOW_EXP
    copies[4].wait()
    for j, g, s in up_slots(groups, up_blocks):
        codes_by_row[pl.ds(j, rows, stride=slots), :] = up_codes[g, :, s * LANES : (s + 1) * LANES]
    for r in range(rows):
        codes = codes_by_row[r * slots : (r + 1) * slots, :]
        values = table
        for bit in range(4):
            odd = (codes & (1 << bit)) != 0
            values = [jnp.where(odd, values[i + 1], values[i]) for i in range(0, len(values), 2)]
        values = values[0]
        out_ref[r] = (values * scales[:, r : r + 1]).astype(jnp.bfloat16)


def chip_sum_kernel(recv, up_global, up_moment, down_global, down_moment, out_ref):
    groups, _, width = up_global.shape
    up_blocks = width // LANES
    for k in range(2):
        total = recv[k].astype(jnp.float32)
        for q in range(1, recv.shape[0] // 2):
            total = total + recv[2 * q + k].astype(jnp.float32)
        out_ref[k] = total
    for j, g, s in up_slots(groups, up_blocks):
        out_ref[2, j : j + 1, :] = up_global[g, :, s * LANES : (s + 1) * LANES]
        out_ref[3, j : j + 1, :] = up_moment[g, :, s * LANES : (s + 1) * LANES]
    for t in range(down_global.shape[1] // LANES):
        j = groups * up_blocks + t
        out_ref[2, j : j + 1, :] = down_global[:, t * LANES : (t + 1) * LANES]
        out_ref[3, j : j + 1, :] = down_moment[:, t * LANES : (t + 1) * LANES]


def advance_kernel(both, out_ref, state, rows_new):
    core = lax.rem(lax.axis_index("replica"), 2)
    replicas = out_ref.shape[0]
    for k in range(2):
        mean = (both[k] + both[4 + k]) / replicas
        moment_new = nesterov * both[4 * k + 3] + mean
        weights_new = both[4 * k + 2] - outer_rate * (mean + nesterov * moment_new)
        shared = weights_new.astype(jnp.bfloat16)
        for q in range(replicas // 2):
            out_ref[2 * q + k] = shared
        rows_new[k, 0] = weights_new
        rows_new[k, 1] = moment_new
    state[...] = rows_new[core]


def merge_kernel(
    recv, up_local, down_local, state, up_merged, down_merged, up_new, up_mom, down_new, down_mom, shared
):
    groups, rows, width = up_local.shape
    up_blocks = width // LANES
    down_blocks = down_local.shape[1] // LANES
    slots = recv.shape[1]
    for r in range(rows):
        shared[r * slots : (r + 1) * slots, :] = recv[r].astype(jnp.float32)

    def merged(local, j):
        theirs = shared[pl.ds(j, rows, stride=slots), :]
        return (mixing * local.astype(jnp.float32) + (1.0 - mixing) * theirs).astype(jnp.bfloat16)

    for j, g, s in up_slots(groups, up_blocks):
        lanes = slice(s * LANES, (s + 1) * LANES)
        up_merged[g, :, lanes] = merged(up_local[g, :, lanes], j)
        up_new[g, :, lanes] = state[0, j : j + 1, :]
        up_mom[g, :, lanes] = state[1, j : j + 1, :]
    for t in range(down_blocks):
        j = groups * up_blocks + t
        lanes = slice(t * LANES, (t + 1) * LANES)
        down_merged[:, lanes] = merged(down_local[:, lanes], j)
        down_new[:, lanes] = state[0, j : j + 1, :]
        down_mom[:, lanes] = state[1, j : j + 1, :]


def per_device(
    code_table,
    up_codes,
    up_exps,
    up_global,
    up_moment,
    up_local,
    down_codes,
    down_exps,
    down_global,
    down_moment,
    down_local,
):
    _, groups, rows, width = up_codes.shape
    depth = down_codes.shape[-1]
    slots = (groups * width + depth) // LANES
    chips = rows // 2
    pairs = [[2 * q, 2 * q + 1] for q in range(chips)]
    sides = [[2 * q + c for q in range(chips)] for c in range(2)]
    first_sides = [[1 - c] + side[1:] for c, side in enumerate(sides)]
    sds = jax.ShapeDtypeStruct
    chunks = sds((rows, slots, LANES), jnp.bfloat16)
    up_exps = jnp.transpose(up_exps[0], (2, 0, 1))
    down_exps = jnp.transpose(down_exps[0], (1, 0))
    streamed = (code_table, up_codes[0], up_exps, down_codes[0], down_exps)
    decoded = pl.pallas_call(
        decode_kernel,
        compiler_params=PARAMS,
        out_shape=chunks,
        in_specs=[HBM] * 5,
        out_specs=VMEM,
        scratch_shapes=[
            pltpu.SMEM(code_table.shape, jnp.int32),
            pltpu.VMEM(up_codes.shape[1:], jnp.int32),
            pltpu.VMEM(up_exps.shape, jnp.int32),
            pltpu.VMEM(down_codes.shape[1:], jnp.int32),
            pltpu.VMEM(down_exps.shape, jnp.int32),
            pltpu.VMEM((rows * slots, LANES), jnp.int32),
            pltpu.VMEM((slots, rows), jnp.int32),
            pltpu.SemaphoreType.DMA((5,)),
        ],
    )(*[pltpu.with_memory_space_constraint(x, pltpu.HBM) for x in streamed])
    recv = lax.all_to_all(
        decoded, "replica", split_axis=0, concat_axis=0, axis_index_groups=first_sides, tiled=True
    )
    mine = pl.pallas_call(
        chip_sum_kernel,
        compiler_params=PARAMS,
        out_shape=sds((4, slots, LANES), jnp.float32),
        in_specs=[VMEM] * 5,
        out_specs=VMEM,
    )(recv, up_global, up_moment, down_global, down_moment)
    both = lax.all_gather(mine, "replica", axis=0, axis_index_groups=pairs, tiled=True)
    shared, state = pl.pallas_call(
        advance_kernel,
        compiler_params=PARAMS,
        out_shape=(chunks, sds((2, slots, LANES), jnp.float32)),
        in_specs=[VMEM],
        out_specs=(VMEM,) * 2,
        scratch_shapes=[pltpu.VMEM((2, 2, slots, LANES), jnp.float32)],
    )(both)
    spread = lax.all_to_all(shared, "replica", split_axis=0, concat_axis=0, axis_index_groups=sides, tiled=True)
    up_merged, down_merged, up_new, up_mom, down_new, down_mom = pl.pallas_call(
        merge_kernel,
        compiler_params=PARAMS,
        out_shape=(
            sds(up_local.shape[1:], jnp.bfloat16),
            sds(down_local.shape[1:], jnp.bfloat16),
            sds(up_global.shape, jnp.float32),
            sds(up_global.shape, jnp.float32),
            sds(down_global.shape, jnp.float32),
            sds(down_global.shape, jnp.float32),
        ),
        in_specs=[VMEM] * 4,
        out_specs=(VMEM,) * 6,
        scratch_shapes=[pltpu.VMEM((rows * slots, LANES), jnp.float32)],
    )(spread, up_local[0], down_local[0], state)
    return (up_new, up_mom, up_merged[None], down_new, down_mom, down_merged[None])


def solution(mesh):
    in_specs = (
        P(),
        P("replica", None, None, "mp"),
        P("replica", None, None, "mp"),
        P(None, "replica", "mp"),
        P(None, "replica", "mp"),
        P("replica", None, None, "mp"),
        P("replica", None, "mp"),
        P("replica", None, "mp"),
        P("replica", "mp"),
        P("replica", "mp"),
        P("replica", None, "mp"),
    )
    out_specs = (
        P(None, "replica", "mp"),
        P(None, "replica", "mp"),
        P("replica", None, None, "mp"),
        P("replica", "mp"),
        P("replica", "mp"),
        P("replica", None, "mp"),
    )
    return jax.shard_map(
        per_device, mesh=mesh, in_specs=in_specs, out_specs=out_specs, check_vma=False
    )
```

```python
import jax
import jax.numpy as jnp
from jax import lax
from jax.experimental import pallas as pl
from jax.experimental.pallas import tpu as pltpu
from jax.sharding import PartitionSpec as P

LANES = 128
LOW_EXP = -8

outer_rate = 0.7
nesterov = 0.9
mixing = 0.5

VMEM = pl.BlockSpec(memory_space=pltpu.VMEM)
HBM = pl.BlockSpec(memory_space=pltpu.HBM)


PARAMS = pltpu.CompilerParams(vmem_limit_bytes=4 * 1024 * 1024)


def up_slots(groups, blocks):
    return [(s * groups + g, g, s) for s in range(blocks) for g in range(groups)]


def decode_kernel(
    table_hbm, up_codes_hbm, up_exps_hbm, down_codes_hbm, down_exps_hbm, out_ref,
    table_ref, up_codes, up_exps, down_codes, down_exps, codes_by_row, exps_by_slot, sems,
):
    copies = [
        pltpu.make_async_copy(source, target, sems.at[i])
        for i, (source, target) in enumerate(
            [
                (table_hbm, table_ref),
                (up_exps_hbm, up_exps),
                (down_exps_hbm, down_exps),
                (down_codes_hbm, down_codes),
                (up_codes_hbm, up_codes),
            ]
        )
    ]
    for copy in reversed(copies):
        copy.start()
    groups, rows, width = up_codes.shape
    up_blocks = width // LANES
    down_blocks = down_codes.shape[1] // LANES
    slots = groups * up_blocks + down_blocks
    copies[0].wait()
    table = [table_ref[level].astype(jnp.float32) for level in range(16)]
    for copy in copies[1:4]:
        copy.wait()
    for j, g, s in up_slots(groups, up_blocks):
        exps_by_slot[j : j + 1, :] = up_exps[s, g : g + 1, :]
    for t in range(down_blocks):
        j = groups * up_blocks + t
        codes_by_row[pl.ds(j, rows, stride=slots), :] = down_codes[:, t * LANES : (t + 1) * LANES]
        exps_by_slot[j : j + 1, :] = down_exps[t : t + 1, :]
    scales = jnp.left_shift(1, exps_by_slot[...] - LOW_EXP).astype(jnp.float32) * 2.0**LOW_EXP
    copies[4].wait()
    for j, g, s in up_slots(groups, up_blocks):
        codes_by_row[pl.ds(j, rows, stride=slots), :] = up_codes[g, :, s * LANES : (s + 1) * LANES]
    for r in range(rows):
        codes = codes_by_row[r * slots : (r + 1) * slots, :]
        values = table
        for bit in range(4):
            odd = (codes & (1 << bit)) != 0
            values = [jnp.where(odd, values[i + 1], values[i]) for i in range(0, len(values), 2)]
        values = values[0]
        out_ref[r] = (values * scales[:, r : r + 1]).astype(jnp.bfloat16)


def chip_sum_kernel(recv, up_global, up_moment, down_global, down_moment, out_ref):
    groups, _, width = up_global.shape
    up_blocks = width // LANES
    for k in range(2):
        total = recv[k].astype(jnp.float32)
        for q in range(1, recv.shape[0] // 2):
            total = total + recv[2 * q + k].astype(jnp.float32)
        out_ref[k] = total
    for j, g, s in up_slots(groups, up_blocks):
        out_ref[2, j : j + 1, :] = up_global[g, :, s * LANES : (s + 1) * LANES]
        out_ref[3, j : j + 1, :] = up_moment[g, :, s * LANES : (s + 1) * LANES]
    for t in range(down_global.shape[1] // LANES):
        j = groups * up_blocks + t
        out_ref[2, j : j + 1, :] = down_global[:, t * LANES : (t + 1) * LANES]
        out_ref[3, j : j + 1, :] = down_moment[:, t * LANES : (t + 1) * LANES]


def advance_kernel(both, out_ref, state, rows_new):
    core = lax.rem(lax.axis_index("replica"), 2)
    replicas = out_ref.shape[0]
    for k in range(2):
        mean = (both[k] + both[4 + k]) / replicas
        moment_new = nesterov * both[4 * k + 3] + mean
        weights_new = both[4 * k + 2] - outer_rate * (mean + nesterov * moment_new)
        shared = weights_new.astype(jnp.bfloat16)
        for q in range(replicas // 2):
            out_ref[2 * q + k] = shared
        rows_new[k, 0] = weights_new
        rows_new[k, 1] = moment_new
    state[...] = rows_new[core]


def merge_kernel(
    recv, up_local, down_local, state, up_merged, down_merged, up_new, up_mom, down_new, down_mom, shared
):
    groups, rows, width = up_local.shape
    up_blocks = width // LANES
    down_blocks = down_local.shape[1] // LANES
    slots = recv.shape[1]
    for r in range(rows):
        shared[r * slots : (r + 1) * slots, :] = recv[r].astype(jnp.float32)

    def merged(local, j):
        theirs = shared[pl.ds(j, rows, stride=slots), :]
        return (mixing * local.astype(jnp.float32) + (1.0 - mixing) * theirs).astype(jnp.bfloat16)

    for j, g, s in up_slots(groups, up_blocks):
        lanes = slice(s * LANES, (s + 1) * LANES)
        up_merged[g, :, lanes] = merged(up_local[g, :, lanes], j)
        up_new[g, :, lanes] = state[0, j : j + 1, :]
        up_mom[g, :, lanes] = state[1, j : j + 1, :]
    for t in range(down_blocks):
        j = groups * up_blocks + t
        lanes = slice(t * LANES, (t + 1) * LANES)
        down_merged[:, lanes] = merged(down_local[:, lanes], j)
        down_new[:, lanes] = state[0, j : j + 1, :]
        down_mom[:, lanes] = state[1, j : j + 1, :]


def per_device(
    code_table,
    up_codes,
    up_exps,
    up_global,
    up_moment,
    up_local,
    down_codes,
    down_exps,
    down_global,
    down_moment,
    down_local,
):
    _, groups, rows, width = up_codes.shape
    depth = down_codes.shape[-1]
    slots = (groups * width + depth) // LANES
    chips = rows // 2
    pairs = [[2 * q, 2 * q + 1] for q in range(chips)]
    sides = [[2 * q + c for q in range(chips)] for c in range(2)]
    first_sides = [[1 - c] + side[1:] for c, side in enumerate(sides)]
    second_sides = [side[:1] + sides[1 - c][1:4] + side[4:] for c, side in enumerate(sides)]
    sds = jax.ShapeDtypeStruct
    chunks = sds((rows, slots, LANES), jnp.bfloat16)
    up_exps = jnp.transpose(up_exps[0], (2, 0, 1))
    down_exps = jnp.transpose(down_exps[0], (1, 0))
    streamed = (code_table, up_codes[0], up_exps, down_codes[0], down_exps)
    decoded = pl.pallas_call(
        decode_kernel,
        compiler_params=PARAMS,
        out_shape=chunks,
        in_specs=[HBM] * 5,
        out_specs=VMEM,
        scratch_shapes=[
            pltpu.SMEM(code_table.shape, jnp.int32),
            pltpu.VMEM(up_codes.shape[1:], jnp.int32),
            pltpu.VMEM(up_exps.shape, jnp.int32),
            pltpu.VMEM(down_codes.shape[1:], jnp.int32),
            pltpu.VMEM(down_exps.shape, jnp.int32),
            pltpu.VMEM((rows * slots, LANES), jnp.int32),
            pltpu.VMEM((slots, rows), jnp.int32),
            pltpu.SemaphoreType.DMA((5,)),
        ],
    )(*[pltpu.with_memory_space_constraint(x, pltpu.HBM) for x in streamed])
    recv = lax.all_to_all(
        decoded, "replica", split_axis=0, concat_axis=0, axis_index_groups=first_sides, tiled=True
    )
    mine = pl.pallas_call(
        chip_sum_kernel,
        compiler_params=PARAMS,
        out_shape=sds((4, slots, LANES), jnp.float32),
        in_specs=[VMEM] * 5,
        out_specs=VMEM,
    )(recv, up_global, up_moment, down_global, down_moment)
    both = lax.all_gather(mine, "replica", axis=0, axis_index_groups=pairs, tiled=True)
    shared, state = pl.pallas_call(
        advance_kernel,
        compiler_params=PARAMS,
        out_shape=(chunks, sds((2, slots, LANES), jnp.float32)),
        in_specs=[VMEM],
        out_specs=(VMEM,) * 2,
        scratch_shapes=[pltpu.VMEM((2, 2, slots, LANES), jnp.float32)],
    )(both)
    spread = lax.all_to_all(
        shared, "replica", split_axis=0, concat_axis=0, axis_index_groups=second_sides, tiled=True
    )
    up_merged, down_merged, up_new, up_mom, down_new, down_mom = pl.pallas_call(
        merge_kernel,
        compiler_params=PARAMS,
        out_shape=(
            sds(up_local.shape[1:], jnp.bfloat16),
            sds(down_local.shape[1:], jnp.bfloat16),
            sds(up_global.shape, jnp.float32),
            sds(up_global.shape, jnp.float32),
            sds(down_global.shape, jnp.float32),
            sds(down_global.shape, jnp.float32),
        ),
        in_specs=[VMEM] * 4,
        out_specs=(VMEM,) * 6,
        scratch_shapes=[pltpu.VMEM((rows * slots, LANES), jnp.float32)],
    )(spread, up_local[0], down_local[0], state)
    return (up_new, up_mom, up_merged[None], down_new, down_mom, down_merged[None])


def solution(mesh):
    in_specs = (
        P(),
        P("replica", None, None, "mp"),
        P("replica", None, None, "mp"),
        P(None, "replica", "mp"),
        P(None, "replica", "mp"),
        P("replica", None, None, "mp"),
        P("replica", None, "mp"),
        P("replica", None, "mp"),
        P("replica", "mp"),
        P("replica", "mp"),
        P("replica", None, "mp"),
    )
    out_specs = (
        P(None, "replica", "mp"),
        P(None, "replica", "mp"),
        P("replica", None, None, "mp"),
        P("replica", "mp"),
        P("replica", "mp"),
        P("replica", None, "mp"),
    )
    return jax.shard_map(
        per_device, mesh=mesh, in_specs=in_specs, out_specs=out_specs, check_vma=False
    )
```

```python
import jax
import jax.numpy as jnp
from jax import lax
from jax.experimental import pallas as pl
from jax.experimental.pallas import tpu as pltpu
from jax.sharding import PartitionSpec as P

LANES = 128
LOW_EXP = -8

outer_rate = 0.7
nesterov = 0.9
mixing = 0.5

VMEM = pl.BlockSpec(memory_space=pltpu.VMEM)
HBM = pl.BlockSpec(memory_space=pltpu.HBM)


PARAMS = pltpu.CompilerParams(vmem_limit_bytes=4 * 1024 * 1024)


def up_slots(groups, blocks):
    return [(s * groups + g, g, s) for s in range(blocks) for g in range(groups)]


def decode_kernel(
    table_hbm, up_codes_hbm, up_exps_hbm, down_codes_hbm, down_exps_hbm, out_ref,
    table_ref, up_codes, up_exps, down_codes, down_exps, codes_by_row, exps_by_slot, sems,
):
    copies = [
        pltpu.make_async_copy(source, target, sems.at[i])
        for i, (source, target) in enumerate(
            [
                (table_hbm, table_ref),
                (up_exps_hbm, up_exps),
                (down_exps_hbm, down_exps),
                (down_codes_hbm, down_codes),
                (up_codes_hbm, up_codes),
            ]
        )
    ]
    for copy in reversed(copies):
        copy.start()
    groups, rows, width = up_codes.shape
    up_blocks = width // LANES
    down_blocks = down_codes.shape[1] // LANES
    slots = groups * up_blocks + down_blocks
    copies[0].wait()
    table = [table_ref[level].astype(jnp.float32) for level in range(16)]
    for copy in copies[1:4]:
        copy.wait()
    for j, g, s in up_slots(groups, up_blocks):
        exps_by_slot[j : j + 1, :] = up_exps[s, g : g + 1, :]
    for t in range(down_blocks):
        j = groups * up_blocks + t
        codes_by_row[pl.ds(j, rows, stride=slots), :] = down_codes[:, t * LANES : (t + 1) * LANES]
        exps_by_slot[j : j + 1, :] = down_exps[t : t + 1, :]
    scales = jnp.left_shift(1, exps_by_slot[...] - LOW_EXP).astype(jnp.float32) * 2.0**LOW_EXP
    copies[4].wait()
    for j, g, s in up_slots(groups, up_blocks):
        codes_by_row[pl.ds(j, rows, stride=slots), :] = up_codes[g, :, s * LANES : (s + 1) * LANES]
    for r in range(rows):
        codes = codes_by_row[r * slots : (r + 1) * slots, :]
        values = table
        for bit in range(4):
            odd = (codes & (1 << bit)) != 0
            values = [jnp.where(odd, values[i + 1], values[i]) for i in range(0, len(values), 2)]
        values = values[0]
        out_ref[(r + rows // 2) % rows] = (values * scales[:, r : r + 1]).astype(jnp.bfloat16)


def chip_sum_kernel(recv, up_global, up_moment, down_global, down_moment, out_ref):
    groups, _, width = up_global.shape
    up_blocks = width // LANES
    for k in range(2):
        total = recv[k].astype(jnp.float32)
        for q in range(1, recv.shape[0] // 2):
            total = total + recv[2 * q + k].astype(jnp.float32)
        out_ref[k] = total
    for j, g, s in up_slots(groups, up_blocks):
        out_ref[2, j : j + 1, :] = up_global[g, :, s * LANES : (s + 1) * LANES]
        out_ref[3, j : j + 1, :] = up_moment[g, :, s * LANES : (s + 1) * LANES]
    for t in range(down_global.shape[1] // LANES):
        j = groups * up_blocks + t
        out_ref[2, j : j + 1, :] = down_global[:, t * LANES : (t + 1) * LANES]
        out_ref[3, j : j + 1, :] = down_moment[:, t * LANES : (t + 1) * LANES]


def advance_kernel(both, out_ref, state, rows_new):
    core = lax.rem(lax.axis_index("replica"), 2)
    replicas = out_ref.shape[0]
    for k in range(2):
        mean = (both[k] + both[4 + k]) / replicas
        moment_new = nesterov * both[4 * k + 3] + mean
        weights_new = both[4 * k + 2] - outer_rate * (mean + nesterov * moment_new)
        shared = weights_new.astype(jnp.bfloat16)
        for q in range(replicas // 2):
            out_ref[2 * q + k] = shared
        rows_new[k, 0] = weights_new
        rows_new[k, 1] = moment_new
    state[...] = rows_new[core]


def merge_kernel(
    recv, up_local, down_local, state, up_merged, down_merged, up_new, up_mom, down_new, down_mom, shared
):
    groups, rows, width = up_local.shape
    up_blocks = width // LANES
    down_blocks = down_local.shape[1] // LANES
    slots = recv.shape[1]
    for r in range(rows):
        shared[r * slots : (r + 1) * slots, :] = recv[(r + rows // 2) % rows].astype(jnp.float32)

    def merged(local, j):
        theirs = shared[pl.ds(j, rows, stride=slots), :]
        return (mixing * local.astype(jnp.float32) + (1.0 - mixing) * theirs).astype(jnp.bfloat16)

    for j, g, s in up_slots(groups, up_blocks):
        lanes = slice(s * LANES, (s + 1) * LANES)
        up_merged[g, :, lanes] = merged(up_local[g, :, lanes], j)
        up_new[g, :, lanes] = state[0, j : j + 1, :]
        up_mom[g, :, lanes] = state[1, j : j + 1, :]
    for t in range(down_blocks):
        j = groups * up_blocks + t
        lanes = slice(t * LANES, (t + 1) * LANES)
        down_merged[:, lanes] = merged(down_local[:, lanes], j)
        down_new[:, lanes] = state[0, j : j + 1, :]
        down_mom[:, lanes] = state[1, j : j + 1, :]


def per_device(
    code_table,
    up_codes,
    up_exps,
    up_global,
    up_moment,
    up_local,
    down_codes,
    down_exps,
    down_global,
    down_moment,
    down_local,
):
    _, groups, rows, width = up_codes.shape
    depth = down_codes.shape[-1]
    slots = (groups * width + depth) // LANES
    chips = rows // 2
    pairs = [[2 * q, 2 * q + 1] for q in range(chips)]
    order = [(q + chips // 2) % chips for q in range(chips)]
    first_sides = [[2 * q + (c if q else 1 - c) for q in order] for c in range(2)]
    second_sides = [[2 * q + c for q in order] for c in range(2)]
    sds = jax.ShapeDtypeStruct
    chunks = sds((rows, slots, LANES), jnp.bfloat16)
    up_exps = jnp.transpose(up_exps[0], (2, 0, 1))
    down_exps = jnp.transpose(down_exps[0], (1, 0))
    streamed = (code_table, up_codes[0], up_exps, down_codes[0], down_exps)
    decoded = pl.pallas_call(
        decode_kernel,
        compiler_params=PARAMS,
        out_shape=chunks,
        in_specs=[HBM] * 5,
        out_specs=VMEM,
        scratch_shapes=[
            pltpu.SMEM(code_table.shape, jnp.int32),
            pltpu.VMEM(up_codes.shape[1:], jnp.int32),
            pltpu.VMEM(up_exps.shape, jnp.int32),
            pltpu.VMEM(down_codes.shape[1:], jnp.int32),
            pltpu.VMEM(down_exps.shape, jnp.int32),
            pltpu.VMEM((rows * slots, LANES), jnp.int32),
            pltpu.VMEM((slots, rows), jnp.int32),
            pltpu.SemaphoreType.DMA((5,)),
        ],
    )(*[pltpu.with_memory_space_constraint(x, pltpu.HBM) for x in streamed])
    recv = lax.all_to_all(
        decoded, "replica", split_axis=0, concat_axis=0, axis_index_groups=first_sides, tiled=True
    )
    mine = pl.pallas_call(
        chip_sum_kernel,
        compiler_params=PARAMS,
        out_shape=sds((4, slots, LANES), jnp.float32),
        in_specs=[VMEM] * 5,
        out_specs=VMEM,
    )(recv, up_global, up_moment, down_global, down_moment)
    both = lax.all_gather(mine, "replica", axis=0, axis_index_groups=pairs, tiled=True)
    shared, state = pl.pallas_call(
        advance_kernel,
        compiler_params=PARAMS,
        out_shape=(chunks, sds((2, slots, LANES), jnp.float32)),
        in_specs=[VMEM],
        out_specs=(VMEM,) * 2,
        scratch_shapes=[pltpu.VMEM((2, 2, slots, LANES), jnp.float32)],
    )(both)
    spread = lax.all_to_all(
        shared, "replica", split_axis=0, concat_axis=0, axis_index_groups=second_sides, tiled=True
    )
    up_merged, down_merged, up_new, up_mom, down_new, down_mom = pl.pallas_call(
        merge_kernel,
        compiler_params=PARAMS,
        out_shape=(
            sds(up_local.shape[1:], jnp.bfloat16),
            sds(down_local.shape[1:], jnp.bfloat16),
            sds(up_global.shape, jnp.float32),
            sds(up_global.shape, jnp.float32),
            sds(down_global.shape, jnp.float32),
            sds(down_global.shape, jnp.float32),
        ),
        in_specs=[VMEM] * 4,
        out_specs=(VMEM,) * 6,
        scratch_shapes=[pltpu.VMEM((rows * slots, LANES), jnp.float32)],
    )(spread, up_local[0], down_local[0], state)
    return (up_new, up_mom, up_merged[None], down_new, down_mom, down_merged[None])


def solution(mesh):
    in_specs = (
        P(),
        P("replica", None, None, "mp"),
        P("replica", None, None, "mp"),
        P(None, "replica", "mp"),
        P(None, "replica", "mp"),
        P("replica", None, None, "mp"),
        P("replica", None, "mp"),
        P("replica", None, "mp"),
        P("replica", "mp"),
        P("replica", "mp"),
        P("replica", None, "mp"),
    )
    out_specs = (
        P(None, "replica", "mp"),
        P(None, "replica", "mp"),
        P("replica", None, None, "mp"),
        P("replica", "mp"),
        P("replica", "mp"),
        P("replica", None, "mp"),
    )
    return jax.shard_map(
        per_device, mesh=mesh, in_specs=in_specs, out_specs=out_specs, check_vma=False
    )
```

```python
import jax
import jax.numpy as jnp
from jax import lax
from jax.experimental import pallas as pl
from jax.experimental.pallas import tpu as pltpu
from jax.sharding import PartitionSpec as P

LANES = 128
LOW_EXP = -8

outer_rate = 0.7
nesterov = 0.9
mixing = 0.5

VMEM = pl.BlockSpec(memory_space=pltpu.VMEM)
HBM = pl.BlockSpec(memory_space=pltpu.HBM)


PARAMS = pltpu.CompilerParams(vmem_limit_bytes=4 * 1024 * 1024)


def up_slots(groups, blocks):
    return [(s * groups + g, g, s) for s in range(blocks) for g in range(groups)]


def decode_kernel(
    table_hbm, up_codes_hbm, up_exps_hbm, down_codes_hbm, down_exps_hbm, out_ref,
    table_ref, up_codes, up_exps, down_codes, down_exps, values_by_row, exps_by_slot, sems,
):
    copies = [
        pltpu.make_async_copy(source, target, sems.at[i])
        for i, (source, target) in enumerate(
            [
                (table_hbm, table_ref),
                (up_exps_hbm, up_exps),
                (down_exps_hbm, down_exps),
                (down_codes_hbm, down_codes),
                (up_codes_hbm, up_codes),
            ]
        )
    ]
    for copy in reversed(copies):
        copy.start()
    groups, rows, width = up_codes.shape
    up_blocks = width // LANES
    down_blocks = down_codes.shape[1] // LANES
    slots = groups * up_blocks + down_blocks
    copies[0].wait()
    table = [table_ref[level].astype(jnp.float32) for level in range(16)]
    def look_up(codes):
        values = table
        for bit in range(4):
            odd = (codes & (1 << bit)) != 0
            values = [jnp.where(odd, values[i + 1], values[i]) for i in range(0, len(values), 2)]
        return values[0]

    for copy in copies[1:4]:
        copy.wait()
    for j, g, s in up_slots(groups, up_blocks):
        exps_by_slot[j : j + 1, :] = up_exps[s, g : g + 1, :]
    for t in range(down_blocks):
        j = groups * up_blocks + t
        values_by_row[pl.ds(j, rows, stride=slots), :] = look_up(down_codes[:, t * LANES : (t + 1) * LANES])
        exps_by_slot[j : j + 1, :] = down_exps[t : t + 1, :]
    scales = jnp.left_shift(1, exps_by_slot[...] - LOW_EXP).astype(jnp.float32) * 2.0**LOW_EXP
    copies[4].wait()
    for j, g, s in up_slots(groups, up_blocks):
        block = up_codes[g, :, s * LANES : (s + 1) * LANES]
        values_by_row[pl.ds(j, rows, stride=slots), :] = look_up(block)
    for r in range(rows):
        values = values_by_row[r * slots : (r + 1) * slots, :]
        out_ref[(r + rows // 2) % rows] = (values * scales[:, r : r + 1]).astype(jnp.bfloat16)


def chip_sum_kernel(recv, up_global, up_moment, down_global, down_moment, out_ref):
    groups, _, width = up_global.shape
    up_blocks = width // LANES
    for k in range(2):
        total = recv[k].astype(jnp.float32)
        for q in range(1, recv.shape[0] // 2):
            total = total + recv[2 * q + k].astype(jnp.float32)
        out_ref[k] = total
    for j, g, s in up_slots(groups, up_blocks):
        out_ref[2, j : j + 1, :] = up_global[g, :, s * LANES : (s + 1) * LANES]
        out_ref[3, j : j + 1, :] = up_moment[g, :, s * LANES : (s + 1) * LANES]
    for t in range(down_global.shape[1] // LANES):
        j = groups * up_blocks + t
        out_ref[2, j : j + 1, :] = down_global[:, t * LANES : (t + 1) * LANES]
        out_ref[3, j : j + 1, :] = down_moment[:, t * LANES : (t + 1) * LANES]


def advance_kernel(both, out_ref, state, rows_new):
    core = lax.rem(lax.axis_index("replica"), 2)
    replicas = out_ref.shape[0]
    for k in range(2):
        mean = (both[k] + both[4 + k]) / replicas
        moment_new = nesterov * both[4 * k + 3] + mean
        weights_new = both[4 * k + 2] - outer_rate * (mean + nesterov * moment_new)
        shared = weights_new.astype(jnp.bfloat16)
        for q in range(replicas // 2):
            out_ref[2 * q + k] = shared
        rows_new[k, 0] = weights_new
        rows_new[k, 1] = moment_new
    state[...] = rows_new[core]


def merge_kernel(
    recv, up_local, down_local, state, up_merged, down_merged, up_new, up_mom, down_new, down_mom, shared
):
    groups, rows, width = up_local.shape
    up_blocks = width // LANES
    down_blocks = down_local.shape[1] // LANES
    slots = recv.shape[1]
    for r in range(rows):
        shared[r * slots : (r + 1) * slots, :] = recv[(r + rows // 2) % rows].astype(jnp.float32)

    def merged(local, j):
        theirs = shared[pl.ds(j, rows, stride=slots), :]
        return (mixing * local.astype(jnp.float32) + (1.0 - mixing) * theirs).astype(jnp.bfloat16)

    for j, g, s in up_slots(groups, up_blocks):
        lanes = slice(s * LANES, (s + 1) * LANES)
        up_merged[g, :, lanes] = merged(up_local[g, :, lanes], j)
        up_new[g, :, lanes] = state[0, j : j + 1, :]
        up_mom[g, :, lanes] = state[1, j : j + 1, :]
    for t in range(down_blocks):
        j = groups * up_blocks + t
        lanes = slice(t * LANES, (t + 1) * LANES)
        down_merged[:, lanes] = merged(down_local[:, lanes], j)
        down_new[:, lanes] = state[0, j : j + 1, :]
        down_mom[:, lanes] = state[1, j : j + 1, :]


def per_device(
    code_table,
    up_codes,
    up_exps,
    up_global,
    up_moment,
    up_local,
    down_codes,
    down_exps,
    down_global,
    down_moment,
    down_local,
):
    _, groups, rows, width = up_codes.shape
    depth = down_codes.shape[-1]
    slots = (groups * width + depth) // LANES
    chips = rows // 2
    pairs = [[2 * q, 2 * q + 1] for q in range(chips)]
    order = [(q + chips // 2) % chips for q in range(chips)]
    first_sides = [[2 * q + (c if q else 1 - c) for q in order] for c in range(2)]
    second_sides = [[2 * q + c for q in order] for c in range(2)]
    sds = jax.ShapeDtypeStruct
    chunks = sds((rows, slots, LANES), jnp.bfloat16)
    up_exps = jnp.transpose(up_exps[0], (2, 0, 1))
    down_exps = jnp.transpose(down_exps[0], (1, 0))
    streamed = (code_table, up_codes[0], up_exps, down_codes[0], down_exps)
    decoded = pl.pallas_call(
        decode_kernel,
        compiler_params=PARAMS,
        out_shape=chunks,
        in_specs=[HBM] * 5,
        out_specs=VMEM,
        scratch_shapes=[
            pltpu.SMEM(code_table.shape, jnp.int32),
            pltpu.VMEM(up_codes.shape[1:], jnp.int32),
            pltpu.VMEM(up_exps.shape, jnp.int32),
            pltpu.VMEM(down_codes.shape[1:], jnp.int32),
            pltpu.VMEM(down_exps.shape, jnp.int32),
            pltpu.VMEM((rows * slots, LANES), jnp.float32),
            pltpu.VMEM((slots, rows), jnp.int32),
            pltpu.SemaphoreType.DMA((5,)),
        ],
    )(*[pltpu.with_memory_space_constraint(x, pltpu.HBM) for x in streamed])
    recv = lax.all_to_all(
        decoded, "replica", split_axis=0, concat_axis=0, axis_index_groups=first_sides, tiled=True
    )
    mine = pl.pallas_call(
        chip_sum_kernel,
        compiler_params=PARAMS,
        out_shape=sds((4, slots, LANES), jnp.float32),
        in_specs=[VMEM] * 5,
        out_specs=VMEM,
    )(recv, up_global, up_moment, down_global, down_moment)
    both = lax.all_gather(mine, "replica", axis=0, axis_index_groups=pairs, tiled=True)
    shared, state = pl.pallas_call(
        advance_kernel,
        compiler_params=PARAMS,
        out_shape=(chunks, sds((2, slots, LANES), jnp.float32)),
        in_specs=[VMEM],
        out_specs=(VMEM,) * 2,
        scratch_shapes=[pltpu.VMEM((2, 2, slots, LANES), jnp.float32)],
    )(both)
    spread = lax.all_to_all(
        shared, "replica", split_axis=0, concat_axis=0, axis_index_groups=second_sides, tiled=True
    )
    up_merged, down_merged, up_new, up_mom, down_new, down_mom = pl.pallas_call(
        merge_kernel,
        compiler_params=PARAMS,
        out_shape=(
            sds(up_local.shape[1:], jnp.bfloat16),
            sds(down_local.shape[1:], jnp.bfloat16),
            sds(up_global.shape, jnp.float32),
            sds(up_global.shape, jnp.float32),
            sds(down_global.shape, jnp.float32),
            sds(down_global.shape, jnp.float32),
        ),
        in_specs=[VMEM] * 4,
        out_specs=(VMEM,) * 6,
        scratch_shapes=[pltpu.VMEM((rows * slots, LANES), jnp.float32)],
    )(spread, up_local[0], down_local[0], state)
    return (up_new, up_mom, up_merged[None], down_new, down_mom, down_merged[None])


def solution(mesh):
    in_specs = (
        P(),
        P("replica", None, None, "mp"),
        P("replica", None, None, "mp"),
        P(None, "replica", "mp"),
        P(None, "replica", "mp"),
        P("replica", None, None, "mp"),
        P("replica", None, "mp"),
        P("replica", None, "mp"),
        P("replica", "mp"),
        P("replica", "mp"),
        P("replica", None, "mp"),
    )
    out_specs = (
        P(None, "replica", "mp"),
        P(None, "replica", "mp"),
        P("replica", None, None, "mp"),
        P("replica", "mp"),
        P("replica", "mp"),
        P("replica", None, "mp"),
    )
    return jax.shard_map(
        per_device, mesh=mesh, in_specs=in_specs, out_specs=out_specs, check_vma=False
    )
```
